32 devices in a mesh: tile: 4 (over y, x), box: 4 (over z), slab: 2 (over core).
Axes of the slice: x: 2, y: 2, z: 4, core: 2. Of those that a mesh axis runs over, the one named last changes fastest.
Arguments:
- les: bfloat16 [1024, 3, 48, 256], P(('tile', 'box'), None, 'slab'), may hold values from -6 to 6
- tile_owner: int32 [80, 25, 1], replicated, may hold values from 0 to 15; in each aligned block of 125 rows (0 to 124, 125 to 249, ..., all dimensions but the last counted through in order) at most 9 rows name the same one
- tile_slot: int32 [80, 25], replicated, may hold values from 0 to 63
- box_offset: int32 [80, 2], P(('tile', 'box')), may hold values from 0 to 127
- plane_deficit: float32 [64, 64, 64], P(('tile', 'box'), 'slab'), may hold values from -2.4 to 2.4
- plane_box: int32 [64, 4], P(('tile', 'box')), may hold values from 0 to 79, as said below
- plane_weight: float32 [64, 4], P(('tile', 'box')), may hold values from 0.5 to 1.5
Outputs:
- inflow: bfloat16 [80, 3, 64, 4096], P(('tile', 'box'), None, 'slab')
The draws below stay inside these ranges and needn't reach their ends.
Inputs may be any that keep to these rules, and one draw needn't show every extreme that they name: tile_owner[b, q, 0] is the device along tile+box that holds patch tile q of box b; over the 125 rows of the boxes of one owner no device is named more than 9 times. `plane_box`: box b belongs to owner b // 5; the 4 boxes of one plane have different owners, and over the planes held by one index of tile+box no owner is named more than 1 times, some owner exactly 1 times.
All inputs are finite; a program needn't handle non-finite values.
Results may differ from the reference program's by a relative error of at most 0.0039.
Values may be sent and summed in bfloat16 or wider, within the bound.
A program may use at most 128 MiB of HBM per device.

```python
import math
import jax
import jax.numpy as jnp
import numpy as np
from jax import lax

BOXN = 64
TS = 16
LZ = 48
TILES_DEV = 64
BOX_DEV = 5
PLANES_DEV = 4
CONTRIB = 4
OWNERS = 16
NB = 80
NT = 1024
NPL = 64
PATCH = 25
NEEDS = 125
SLOTS = 9


def draw_plane_box(key, part):
    blocks = NPL // PLANES_DEV
    per_block = PLANES_DEV * CONTRIB
    block_keys = jax.random.split(jax.random.fold_in(key, 11), blocks)
    orders = jax.vmap(lambda k: jax.random.permutation(k, OWNERS))(block_keys)
    cycled = jnp.arange(per_block, dtype=jnp.int32) % OWNERS
    owner_ids = orders[:, cycled].astype(jnp.int32)
    inner = jax.random.randint(jax.random.fold_in(key, 12), (blocks, per_block), 0, BOX_DEV).astype(jnp.int32)
    return (owner_ids * BOX_DEV + inner).reshape(NPL, CONTRIB).astype(jnp.int32)


def with_ends(values, own_key, low, high):
    longest = values.shape.index(max(values.shape))
    spots = []
    for shift in (0, 1):
        where = [jax.random.randint(jax.random.fold_in(own_key, axis), (), 0, length) for axis, length in enumerate(values.shape)]
        where[longest] = (where[longest] + shift) % values.shape[longest]
        spots.append(tuple(where))
    return values.at[spots[0]].set(low).at[spots[1]].set(high)


def block_levels(own_key, extent, shards, low, high):
    def one(axis_at, shards_of):
        draws = jax.random.uniform(jax.random.fold_in(jax.random.fold_in(own_key, 6), axis_at), (shards_of,), jnp.float32, low / len(shards), high / len(shards))
        return jnp.repeat(jnp.exp(draws), extent[axis_at] // shards_of).reshape((-1,) + (1,) * (len(extent) - axis_at - 1))

    factor_of = one(*shards[0])
    for cut in shards[1:]:
        factor_of = factor_of * one(*cut)
    return factor_of


def deal_out(stream_key, own, number, rows, amount, top, reach, skew):
    ranking = jax.random.permutation(stream_key, amount)
    crowded, common = portions_of(amount, rows * top, reach, skew, True), portions_of(amount, rows * top, reach, skew, False)
    places = jnp.arange(amount)

    def named(tallies, offset_by):
        used = int((tallies > 0).sum())
        fixed = max(1, used // 4)
        passed = fixed + (places - fixed + offset_by * (used - fixed)) % max(1, amount - fixed)
        return jnp.zeros((amount,), jnp.int32).at[ranking[jnp.where(places < fixed, places, passed)]].set(jnp.asarray(tallies, jnp.int32))

    tallies = jnp.where(number % 4 == 0, named(crowded, number // 4), named(common, number - number // 4 - 1))
    mixed = jax.random.permutation(jax.random.fold_in(own, 3), amount)
    giver, taker = mixed[0:amount // 2 * 2:2], mixed[1:amount // 2 * 2:2]
    slack = jnp.minimum(tallies[giver] - 1, reach - tallies[taker]) // 2
    slack = jnp.where((giver == ranking[0]) | (taker == ranking[0]) | (tallies[taker] == 0), 0, jnp.maximum(slack, 0))
    passed = jax.random.randint(jax.random.fold_in(own, 4), (amount // 2,), 0, 1 << 20) % (slack + 1)
    tallies = tallies.at[giver].add(-passed).at[taker].add(passed)
    members = jnp.searchsorted(jnp.cumsum(tallies), jnp.arange(rows * top), side="right").astype(jnp.int32)
    listing = members.reshape(top, rows).T
    listing = listing[jax.random.permutation(jax.random.fold_in(own, 1), rows)]
    offset_by = jax.random.randint(jax.random.fold_in(own, 2), (rows, 1), 0, top)
    return jnp.take_along_axis(listing, (jnp.arange(top)[None, :] + offset_by) % top, axis=1)


def portions_of(number_of, total, bound, lean, full):
    loads = [(1 << 20) // math.isqrt(rank ** lean) + 1 for rank in range(1, number_of + 1)]
    largest = bound if full else min(bound, max(-(-total // number_of), total * loads[0] // sum(loads)))
    least = 1 if total - largest >= number_of - 1 else 0
    counts, spare = [largest] + [least] * (number_of - 1), total - largest - least * (number_of - 1)
    while spare > 0:
        candidates = [i for i in range(1, number_of) if counts[i] < largest] or [i for i in range(1, number_of) if counts[i] < bound]
        mass, remaining = sum([loads[i] for i in candidates]), spare
        for i in candidates:
            addition = min(bound - counts[i], max(1, remaining * loads[i] // mass), spare)
            counts[i] = counts[i] + addition
            spare = spare - addition
    return np.array(counts)


def centred(stream_key, shape, deviation, most, shards=(), held_as=jnp.bfloat16):
    gain = block_levels(stream_key, shape, shards, -0.22, 0.18) if shards else 1.0
    result = jax.random.normal(stream_key, shape, jnp.float32) * deviation * gain
    return jnp.minimum(jnp.maximum(result, -most), most).astype(held_as)


def setup_inputs(seed: int = 0) -> dict:
    splits = jax.random.split(jax.random.key(seed), 8)
    les = centred(splits[0], (NT, 3, LZ, TS * TS), 1.0, 6.0, ((0, 16), (2, 2)))
    tile_owner_keys = jax.random.split(jax.random.fold_in(splits[1], 1), NB * PATCH // NEEDS)
    tile_owner_turns = jax.random.permutation(jax.random.fold_in(splits[1], 3), NB * PATCH // NEEDS)
    tile_owner = jax.vmap(lambda own, number: deal_out(jax.random.fold_in(splits[1], 2), own, number, NEEDS, OWNERS, 1, SLOTS, 2))(tile_owner_keys, tile_owner_turns).reshape((NB, PATCH, 1))
    tile_slot = with_ends(jax.random.randint(splits[2], (NB, PATCH), 0, TILES_DEV), jax.random.fold_in(splits[2], 1), 0, TILES_DEV - 1).astype(jnp.int32)
    box_offset = with_ends(jax.random.randint(splits[3], (NB, 2), 0, 8 * TS), jax.random.fold_in(splits[3], 1), 0, (8 * TS) - 1).astype(jnp.int32)
    plane_deficit = centred(splits[4], (NPL, BOXN, BOXN), 0.4, 2.4, ((0, 16), (1, 2)), jnp.float32)
    plane_box = draw_plane_box(jax.random.fold_in(splits[7], 71), 0)
    plane_weight = jnp.clip(0.5 + 1.0 * jax.random.uniform(splits[6], (NPL, CONTRIB), jnp.float32) ** block_levels(splits[6], (NPL, CONTRIB), ((0, 16),), -0.2, 0.2), 0.5, 1.5)
    return dict(les=les, tile_owner=tile_owner, tile_slot=tile_slot, box_offset=box_offset, plane_deficit=plane_deficit, plane_box=plane_box, plane_weight=plane_weight)


FILTER_NU = 0.125


def blend_plane(region, offset):
    count = region.shape[1]
    width = region.shape[3]
    shift_x = offset[0] // 8
    share_x = (offset[0] % 8).astype(jnp.float32) / 8.0
    shift_y = offset[1] // 8
    share_y = (offset[1] % 8).astype(jnp.float32) / 8.0
    zero = jnp.zeros((), jnp.int32)
    left_part = lax.dynamic_slice(region, (zero, zero, zero, shift_x), (3, count, width, BOXN))
    right_part = lax.dynamic_slice(region, (zero, zero, zero, shift_x + 1), (3, count, width, BOXN))
    along_x = (1.0 - share_x) * left_part + share_x * right_part
    front_part = lax.dynamic_slice(along_x, (zero, zero, shift_y, zero), (3, count, BOXN, BOXN))
    back_part = lax.dynamic_slice(along_x, (zero, zero, shift_y + 1, zero), (3, count, BOXN, BOXN))
    return (1.0 - share_y) * front_part + share_y * back_part


def smooth_box(box_flow):
    padded = jnp.pad(box_flow, ((0, 0), (1, 1), (1, 1), (1, 1)), mode="edge")
    center = padded[:, 1:-1, 1:-1, 1:-1]
    stencil_sum = (padded[:, :-2, 1:-1, 1:-1] - center) + (padded[:, 2:, 1:-1, 1:-1] - center)
    stencil_sum = stencil_sum + (padded[:, 1:-1, :-2, 1:-1] - center) + (padded[:, 1:-1, 2:, 1:-1] - center)
    stencil_sum = stencil_sum + (padded[:, 1:-1, 1:-1, :-2] - center) + (padded[:, 1:-1, 1:-1, 2:] - center)
    return center + FILTER_NU * stencil_sum


def reference(les, tile_owner, tile_slot, box_offset, plane_deficit, plane_box, plane_weight):
    patch_side = BOXN // TS + 1
    width = patch_side * TS
    box_total = tile_owner.shape[0]
    points = jnp.arange(BOXN, dtype=jnp.int32)
    level_num = points * (LZ - 1)
    level_low = level_num // (BOXN - 1)
    level_frac = (level_num % (BOXN - 1)).astype(jnp.float32) / float(BOXN - 1)
    deficit_terms = plane_weight[:, :, None, None] * plane_deficit[:, None, :, :]
    wake_loss = jax.ops.segment_sum(deficit_terms.reshape(-1, BOXN, BOXN), plane_box.reshape(-1), num_segments=box_total)

    def one_box(packed):
        owner_row, slot_row, offset, box_loss = packed
        tile_ids = (owner_row * TILES_DEV + slot_row).astype(jnp.int32)
        patch_tiles = jnp.take(les, tile_ids, axis=0)
        top_level = jnp.zeros((patch_tiles.shape[0], 3, 1, TS * TS), patch_tiles.dtype)
        patch_tiles = jnp.concatenate([patch_tiles, top_level], axis=2)
        patch_tiles = patch_tiles.reshape(patch_side, patch_side, 3, LZ + 1, TS, TS)
        region = jnp.transpose(patch_tiles, (2, 3, 0, 4, 1, 5)).reshape(3, LZ + 1, width, width).astype(jnp.float32)
        plane = blend_plane(region, offset)
        lower_plane = jnp.take(plane, level_low, axis=1)
        upper_plane = jnp.take(plane, level_low + 1, axis=1)
        weight = level_frac[None, :, None, None]
        velocity = (1.0 - weight) * lower_plane + weight * upper_plane
        velocity = velocity.at[0].add(-box_loss[:, :, None])
        box_flow = lax.optimization_barrier(velocity.astype(jnp.bfloat16)).astype(jnp.float32)
        return smooth_box(box_flow).astype(jnp.bfloat16).reshape(3, BOXN, BOXN * BOXN)

    return lax.map(one_box, (tile_owner[:, :, 0], tile_slot, box_offset, wake_loss))
```

```python
import jax
import jax.numpy as jnp
from jax import lax
from jax.experimental import pallas as pl
from jax.experimental.pallas import tpu as pltpu
from jax.sharding import PartitionSpec as P

BOXN = 64
TS = 16
LZ = 48
SIDE = BOXN // TS + 1
CELLS = TS * TS
FILTER_NU = 0.125
BF = jnp.bfloat16
F32 = jnp.float32


def iota(shape, dim):
    return lax.broadcasted_iota(jnp.int32, shape, dim)


def send_kernel(slots, box_count, picked, boxes, weights, ext, lower, upper, out):
    owner = pl.program_id(0)
    planes = lower.shape[0]
    contrib = weights.shape[1]
    first = jnp.zeros(lower.shape[1:], F32)
    second = jnp.zeros(lower.shape[1:], F32)
    inner = jnp.int32(0)
    for p in range(planes):
        gain = F32(0.0)
        for e in range(contrib):
            box = boxes[p * contrib + e]
            mine = (box // box_count) == owner
            gain = gain + jnp.where(mine, weights[p, e], F32(0.0))
            inner = inner + jnp.where(mine, box % box_count, 0)
        first = first + gain * lower[p]
        second = second + gain * upper[p]
    row, lane = iota(first.shape, 0), iota(first.shape, 1)
    tag = jnp.full(first.shape, inner, jnp.int32).astype(F32)
    first = jnp.where((row == 12) & (lane >= 128), tag, first)
    for q in range(slots):
        tile = picked[owner * slots + q]
        if q < 2:
            out[q, 0:64, :] = ext[tile, 0:64, :]
            extra = first if q == 0 else second
            out[q, 64:80, :] = (ext[tile, 64:80, :].astype(F32) + extra).astype(BF)
        else:
            out[q] = ext[tile]


def box_kernel(slots, need, offset, got, heights, perm, out, loss_ref, flow):
    b = pl.program_id(0)
    slab = lax.axis_index("slab")
    owners = got.shape[0] // slots
    rows = heights.shape[0]
    levels = out.shape[2]
    total = jnp.zeros((32, CELLS), F32)
    for o in range(owners):
        one = got[o * slots, 64:80, :].astype(F32)
        two = got[o * slots + 1, 64:80, :].astype(F32)
        hit = one[12:13, 128:129] == b.astype(F32)
        total = total + jnp.where(hit, jnp.concatenate([one, two], axis=0), 0.0)
    shape = (rows, 32)
    k, r = iota(shape, 0), iota(shape, 1)
    part = k // 4
    source = jnp.where(k < levels, jnp.where(part < 4, part + 8, part + 20), jnp.where(k == 3 * levels, 12, -1))
    spread = jnp.dot(
        (source == r).astype(F32), total, precision=lax.Precision.HIGHEST, preferred_element_type=F32
    )
    k, lane = iota((rows, CELLS), 0), iota((rows, CELLS), 1)
    want = jnp.where(k < levels, k % 4, 0)
    spread = jnp.where(lane // BOXN == want, spread, 0.0)
    spread_hi = spread.astype(BF)
    spread_lo = (spread - spread_hi.astype(F32)).astype(BF)
    shape = (CELLS, CELLS)
    src, dst = iota(shape, 0), iota(shape, 1)
    for J in range(SIDE - 1):
        expand = (src % BOXN == dst // TS + J * TS).astype(F32).astype(BF)
        loss_ref[J] = jnp.dot(spread_hi, expand, preferred_element_type=F32) + jnp.dot(
            spread_lo, expand, preferred_element_type=F32
        )
    off_x, off_y = offset[2 * b], offset[2 * b + 1]

    def blend(delta, off):
        shift = off // 8
        share = (off % 8).astype(F32) / 8.0
        return jnp.where(delta == shift, 1.0 - share, jnp.where(delta == shift + 1, share, 0.0))

    gap_y, gap_x = src // TS - dst // TS, src % TS - dst % TS
    in_y = [blend(gap_y + d * TS, off_y) for d in (0, 1)]
    in_x = [blend(gap_x + d * TS, off_x) for d in (0, 1)]
    weights = jnp.concatenate([(in_y[i] * in_x[j]).astype(BF) for i in (0, 1) for j in (0, 1)], axis=0)
    levels_hl = heights[...]
    for J in range(SIDE - 1):
        tiles = [[got[need[b * SIDE * SIDE + (J + i) * SIDE + s]] for s in range(SIDE)] for i in (0, 1)]
        left = jnp.concatenate(
            [
                jnp.concatenate([tiles[0][I], tiles[0][I + 1], tiles[1][I], tiles[1][I + 1]], axis=1)
                for I in range(SIDE - 1)
            ],
            axis=0,
        )
        plane = jnp.dot(left, weights, preferred_element_type=F32)
        count = tiles[0][0].shape[0]
        blocks = []
        for I in range(SIDE - 1):
            part = plane[I * count : (I + 1) * count]
            high = part.astype(BF)
            low = (part - high.astype(F32)).astype(BF)
            stack = jnp.concatenate([high, high, low], axis=0)
            blocks.append(
                (jnp.dot(levels_hl, stack, preferred_element_type=F32) - loss_ref[J]).astype(BF)
            )
        flow[:, J * 1024 : (J + 1) * 1024] = jnp.dot(
            jnp.concatenate(blocks, axis=1), perm[...], preferred_element_type=F32
        )
    points = BOXN * BOXN
    shape = (levels, points)
    row, lane = iota(shape, 0), iota(shape, 1)
    for c in range(3):
        center = flow[c * levels : (c + 1) * levels, :]
        beside = jnp.broadcast_to(flow[3 * levels + c : 3 * levels + c + 1, :], shape)
        down = jnp.where(row == 0, jnp.where(slab == 0, center, beside), pltpu.roll(center, 1, 0))
        up = jnp.where(
            row == levels - 1, jnp.where(slab == 0, beside, center), pltpu.roll(center, levels - 1, 0)
        )
        total = down + up
        total = total + jnp.where(lane < BOXN, center, pltpu.roll(center, BOXN, 1))
        total = total + jnp.where(lane >= points - BOXN, center, pltpu.roll(center, points - BOXN, 1))
        total = total + jnp.where(lane % BOXN == 0, center, pltpu.roll(center, 1, 1))
        total = total + jnp.where(lane % BOXN == BOXN - 1, center, pltpu.roll(center, points - 1, 1))
        out[0, c] = (center + FILTER_NU * (total - 6.0 * center)).astype(BF)


def body(les, tile_owner, tile_slot, box_offset, plane_deficit, plane_box, plane_weight):
    owners = lax.axis_size(("tile", "box"))
    my_index = lax.axis_index(("tile", "box"))
    slab = lax.axis_index("slab")
    tile_count, _, slab_levels, _ = les.shape
    patch_count = tile_owner.shape[1]
    box_count = box_offset.shape[0]
    need_count = box_count * patch_count
    slots = (need_count + owners - 1) // owners + 1
    sources = tile_owner[:, :, 0].reshape(owners, need_count)
    local_tiles = tile_slot.reshape(owners, need_count)
    from_here = (sources == my_index).astype(jnp.int32)
    slot_rank = jnp.cumsum(from_here, axis=1) - from_here
    slot_ids = jnp.arange(slots, dtype=jnp.int32)
    chosen = (from_here[:, None, :] == 1) & (slot_rank[:, None, :] == slot_ids[None, :, None])
    picked = jnp.sum(jnp.where(chosen, local_tiles[:, None, :], 0), axis=2).reshape(-1)
    wanted = lax.dynamic_slice_in_dim(sources, my_index, 1, 0)[0]
    need_ids = jnp.arange(need_count, dtype=jnp.int32)
    same_source = (wanted[:, None] == wanted[None, :]) & (need_ids[None, :] < need_ids[:, None])
    slot_of = jnp.sum(same_source.astype(jnp.int32), axis=1)
    need = wanted * slots + slot_of

    planes, points, _ = plane_deficit.shape
    edge = jnp.where(slab == 0, les[:, :, slab_levels - 1], les[:, :, 0]).reshape(-1, CELLS)
    rim = jnp.where(slab == 0, plane_deficit[:, points - 1], plane_deficit[:, 0]).reshape(-1, CELLS)
    rim_hi = lax.reduce_precision(rim, 8, 7)
    rim_lo = rim - rim_hi
    payload = jnp.concatenate([edge, rim_hi.astype(BF), rim_lo.astype(BF)], axis=0)
    payload = lax.ppermute(payload, "slab", [(0, 1), (1, 0)])
    edge_rows = tile_count * 3
    edge = payload[:edge_rows].reshape(tile_count, 3, CELLS)
    rim_rows = rim.shape[0]
    rim = payload[edge_rows : edge_rows + rim_rows].astype(F32) + payload[edge_rows + rim_rows :].astype(F32)
    rim = rim.reshape(planes, 1, BOXN)
    band = 3 * slab_levels
    ext = jnp.concatenate(
        [les.reshape(tile_count, band, CELLS), jnp.zeros((tile_count, 5, CELLS), BF), edge], axis=1
    )
    count = ext.shape[1]
    flat = plane_deficit.reshape(planes, points * BOXN // CELLS, CELLS)
    zero = jnp.zeros((planes, 8, CELLS), F32)
    rim = jnp.pad(rim, ((0, 0), (0, 0), (0, CELLS - BOXN)))
    lower = jnp.concatenate([zero, flat[:, :4], rim, zero[:, :3]], axis=1)
    upper = jnp.concatenate([zero, flat[:, 4:], zero[:, :4]], axis=1)

    smem = pl.BlockSpec(memory_space=pltpu.SMEM)
    outgoing = pl.pallas_call(
        lambda *refs: send_kernel(slots, box_count, *refs),
        grid=(owners,),
        in_specs=[
            smem,
            smem,
            smem,
            pl.BlockSpec((tile_count, count, CELLS), lambda o: (0, 0, 0)),
            pl.BlockSpec((planes, 16, CELLS), lambda o: (0, 0, 0)),
            pl.BlockSpec((planes, 16, CELLS), lambda o: (0, 0, 0)),
        ],
        out_specs=pl.BlockSpec((slots, count, CELLS), lambda o: (o, 0, 0)),
        out_shape=jax.ShapeDtypeStruct((owners * slots, count, CELLS), BF),
        compiler_params=pltpu.CompilerParams(vmem_limit_bytes=32 << 20),
        name="pick_tiles",
    )(picked, plane_box.reshape(-1), plane_weight, ext, lower, upper)
    got = lax.all_to_all(outgoing, ("tile", "box"), split_axis=0, concat_axis=0, tiled=True)

    rows = 3 * points + 8
    row = jnp.arange(rows, dtype=jnp.int32)[:, None]
    comp = jnp.where(row < 3 * points, row // points, row - 3 * points)
    height = jnp.where(
        row < 3 * points, slab * points + row % points, jnp.where(slab == 0, points, points - 1)
    )
    num = height * (LZ - 1)
    low = num // (BOXN - 1)
    frac = (num % (BOXN - 1)).astype(F32) / float(BOXN - 1)
    col = jnp.arange(count, dtype=jnp.int32)[None, :]
    other = jnp.where(slab == 0, slab_levels, slab_levels - 1)
    col_level = jnp.where(col < band, slab * slab_levels + col % slab_levels, other)
    col_comp = jnp.where(col < band, col // slab_levels, jnp.where(col >= band + 5, col - band - 5, 7))
    mix = jnp.where(col_level == low, 1.0 - frac, jnp.where(col_level == low + 1, frac, 0.0))
    mix = jnp.where((col_comp == comp) & (comp < 3), mix, 0.0)
    mix_hi = lax.reduce_precision(mix, 8, 7)
    mix_lo = mix - mix_hi
    heights = jnp.concatenate([mix_hi, mix_lo, mix_hi], axis=1).astype(BF)
    wide = TS * BOXN
    lane = jnp.arange(wide, dtype=jnp.int32)
    to = (lane % CELLS // TS) * BOXN + (lane // CELLS) * TS + lane % TS
    perm = (to[:, None] == lane[None, :]).astype(BF)

    return pl.pallas_call(
        lambda *refs: box_kernel(slots, *refs),
        grid=(box_count,),
        in_specs=[
            smem,
            smem,
            pl.BlockSpec((owners * slots, count, CELLS), lambda b: (0, 0, 0)),
            pl.BlockSpec((rows, 3 * count), lambda b: (0, 0)),
            pl.BlockSpec((wide, wide), lambda b: (0, 0)),
        ],
        out_specs=pl.BlockSpec((1, 3, points, BOXN * BOXN), lambda b: (b, 0, 0, 0)),
        out_shape=jax.ShapeDtypeStruct((box_count, 3, points, BOXN * BOXN), BF),
        scratch_shapes=[
            pltpu.VMEM((SIDE - 1, rows, CELLS), F32),
            pltpu.VMEM((rows, BOXN * BOXN), F32),
        ],
        compiler_params=pltpu.CompilerParams(vmem_limit_bytes=56 << 20),
        name="interpolate_smooth",
    )(need, box_offset.reshape(-1), got, heights, perm)


def solution(mesh):
    placed = (
        P(("tile", "box"), None, "slab", None),
        P(),
        P(),
        P(("tile", "box"), None),
        P(("tile", "box"), "slab", None),
        P(("tile", "box"), None),
        P(("tile", "box"), None),
    )
    return jax.shard_map(
        body,
        mesh=mesh,
        in_specs=placed,
        out_specs=P(("tile", "box"), None, "slab", None),
        check_vma=False,
    )
```

```python
import jax
import jax.numpy as jnp
from jax import lax
from jax.experimental import pallas as pl
from jax.experimental.pallas import tpu as pltpu
from jax.sharding import PartitionSpec as P

BOXN = 64
TS = 16
LZ = 48
SIDE = BOXN // TS + 1
CELLS = TS * TS
FILTER_NU = 0.125
BF = jnp.bfloat16
F32 = jnp.float32


def iota(shape, dim):
    return lax.broadcasted_iota(jnp.int32, shape, dim)


def pick_kernel(slots, picked, les, out):
    owner = pl.program_id(0)
    for q in range(slots):
        out[q] = les[picked[owner * slots + q], 0]


def box_kernel(comp, need, offset, got, edge, wake, heights, perm, *rest):
    out, region, flow = rest[-3:]
    b = pl.program_id(0)
    slab = lax.axis_index("slab")
    rows = heights.shape[0]
    levels = out.shape[2]
    blocks = SIDE - 1
    shape = (CELLS, CELLS)
    src, dst = iota(shape, 0), iota(shape, 1)
    if comp == 0:
        total = jnp.zeros(wake.shape[1:], F32)
        for o in range(wake.shape[0]):
            one = wake[o]
            total = total + jnp.where(one[8:9, 128:129] == b.astype(F32), one, 0.0)
        k, r = iota((rows, total.shape[0]), 0), iota((rows, total.shape[0]), 1)
        source = jnp.where(k < levels, k // 4, jnp.where(k == levels, 9, -1))
        spread = jnp.dot(
            (source == r).astype(F32), total, precision=lax.Precision.HIGHEST, preferred_element_type=F32
        )
        k, lane = iota((rows, CELLS), 0), iota((rows, CELLS), 1)
        spread = jnp.where(lane // BOXN == jnp.where(k < levels, k % 4, 0), spread, 0.0)
        spread_hi = spread.astype(BF)
        spread_lo = (spread - spread_hi.astype(F32)).astype(BF)
    off_x, off_y = offset[2 * b], offset[2 * b + 1]

    def blend(delta, off):
        shift = off // 8
        share = (off % 8).astype(F32) / 8.0
        return jnp.where(delta == shift, 1.0 - share, jnp.where(delta == shift + 1, share, 0.0))

    gap_y, gap_x = src // TS - dst // TS, src % TS - dst % TS
    in_y = [blend(gap_y + d * TS, off_y) for d in (0, 1)]
    in_x = [blend(gap_x + d * TS, off_x) for d in (0, 1)]
    weights = jnp.concatenate([(in_y[i] * in_x[j]).astype(BF) for i in (0, 1) for j in (0, 1)], axis=0)
    for q in range(SIDE * SIDE):
        tile = need[b * SIDE * SIDE + q]
        both = jnp.concatenate([got[tile].astype(F32), edge[tile].astype(F32)], axis=0)
        region[q] = both.astype(BF)
    count = region.shape[1]
    left = jnp.concatenate(
        [
            jnp.concatenate([region[(J + i) * SIDE + I + j] for i in (0, 1) for j in (0, 1)], axis=1)
            for J in range(blocks)
            for I in range(blocks)
        ],
        axis=0,
    )
    plane = jnp.dot(left, weights, preferred_element_type=F32)
    levels_hl = heights[...]
    bands = []
    for J in range(blocks):
        if comp == 0:
            expand = (src % BOXN == dst // TS + J * TS).astype(F32).astype(BF)
            loss = jnp.dot(spread_hi, expand, preferred_element_type=F32) + jnp.dot(
                spread_lo, expand, preferred_element_type=F32
            )
        band = []
        for I in range(blocks):
            at = (J * blocks + I) * count
            part = plane[at : at + count]
            high = part.astype(BF)
            low = (part - high.astype(F32)).astype(BF)
            stack = jnp.concatenate([high, high, low], axis=0)
            value = jnp.dot(levels_hl, stack, preferred_element_type=F32)
            band.append((value - loss if comp == 0 else value).astype(BF))
        bands.append(jnp.concatenate(band, axis=1))
    flow[...] = jnp.dot(jnp.concatenate(bands, axis=0), perm[...], preferred_element_type=F32)
    points = BOXN * BOXN
    shape = (levels, points)
    row, lane = iota(shape, 0), iota(shape, 1)
    center = jnp.concatenate([flow[J * rows : J * rows + levels, :] for J in range(blocks)], axis=1)
    beside = jnp.concatenate(
        [flow[J * rows + levels : J * rows + levels + 1, :] for J in range(blocks)], axis=1
    )
    beside = jnp.broadcast_to(beside, shape)
    down = jnp.where(row == 0, jnp.where(slab == 0, center, beside), pltpu.roll(center, 1, 0))
    up = jnp.where(
        row == levels - 1, jnp.where(slab == 0, beside, center), pltpu.roll(center, levels - 1, 0)
    )
    total = down + up
    total = total + jnp.where(lane < BOXN, center, pltpu.roll(center, BOXN, 1))
    total = total + jnp.where(lane >= points - BOXN, center, pltpu.roll(center, points - BOXN, 1))
    total = total + jnp.where(lane % BOXN == 0, center, pltpu.roll(center, 1, 1))
    total = total + jnp.where(lane % BOXN == BOXN - 1, center, pltpu.roll(center, points - 1, 1))
    out[0, 0] = (center + FILTER_NU * (total - 6.0 * center)).astype(BF)


def body(les, tile_owner, tile_slot, box_offset, plane_deficit, plane_box, plane_weight):
    owners = lax.axis_size(("tile", "box"))
    my_index = lax.axis_index(("tile", "box"))
    slab = lax.axis_index("slab")
    tile_count, comps, slab_levels, _ = les.shape
    patch_count = tile_owner.shape[1]
    box_count = box_offset.shape[0]
    planes, points, _ = plane_deficit.shape
    need_count = box_count * patch_count
    slots = (need_count + owners - 1) // owners + 1
    total_slots = owners * slots
    sources = tile_owner[:, :, 0].reshape(owners, need_count)
    local_tiles = tile_slot.reshape(owners, need_count)
    from_here = (sources == my_index).astype(jnp.int32)
    slot_rank = jnp.cumsum(from_here, axis=1) - from_here
    slot_ids = jnp.arange(slots, dtype=jnp.int32)
    chosen = (from_here[:, None, :] == 1) & (slot_rank[:, None, :] == slot_ids[None, :, None])
    picked = jnp.sum(jnp.where(chosen, local_tiles[:, None, :], 0), axis=2).reshape(-1)
    wanted = lax.dynamic_slice_in_dim(sources, my_index, 1, 0)[0]
    need_ids = jnp.arange(need_count, dtype=jnp.int32)
    same_source = (wanted[:, None] == wanted[None, :]) & (need_ids[None, :] < need_ids[:, None])
    slot_of = jnp.sum(same_source.astype(jnp.int32), axis=1)
    need = wanted * slots + slot_of
    group = ("tile", "box")
    swap = [(0, 1), (1, 0)]
    smem = pl.BlockSpec(memory_space=pltpu.SMEM)

    theirs = plane_box[None] // box_count == jnp.arange(owners, dtype=jnp.int32)[:, None, None]
    gain = jnp.sum(jnp.where(theirs, plane_weight[None], 0.0), axis=2)
    tag = jnp.sum(jnp.where(theirs, plane_box[None] % box_count, 0), axis=(1, 2)).astype(F32)
    flat = plane_deficit.reshape(planes, points * BOXN // CELLS, CELLS)
    terms = gain[:, 0, None, None] * flat[0]
    for p in range(1, planes):
        terms = terms + gain[:, p, None, None] * flat[p]
    flat_rows = flat.shape[1]
    tags = jnp.broadcast_to(tag[:, None, None], (owners, 16 - flat_rows, CELLS))
    wake = lax.all_to_all(
        jnp.concatenate([terms, tags], axis=1).astype(BF), group, split_axis=0, concat_axis=0, tiled=True
    )
    rim = jnp.where(slab == 0, wake[:, flat_rows - 1, CELLS - BOXN :], wake[:, 0, :BOXN])
    rim = lax.ppermute(rim, "slab", swap)
    wake = wake.astype(F32).at[:, 9, :BOXN].set(rim.astype(F32))

    rows = points + 16
    count = slab_levels + 8
    row = jnp.arange(rows, dtype=jnp.int32)[:, None]
    height = jnp.where(row < points, slab * points + row, jnp.where(slab == 0, points, points - 1))
    num = height * (LZ - 1)
    low = num // (BOXN - 1)
    frac = (num % (BOXN - 1)).astype(F32) / float(BOXN - 1)
    col = jnp.arange(count, dtype=jnp.int32)[None, :]
    col_level = jnp.where(
        col < slab_levels, slab * slab_levels + col, jnp.where(slab == 0, col, col - 8)
    )
    mix = jnp.where(col_level == low, 1.0 - frac, jnp.where(col_level == low + 1, frac, 0.0))
    mix = jnp.where(row <= points, mix, 0.0)
    mix_hi = lax.reduce_precision(mix, 8, 7)
    mix_lo = mix - mix_hi
    heights = jnp.concatenate([mix_hi, mix_lo, mix_hi], axis=1).astype(BF)
    wide = TS * BOXN
    lane = jnp.arange(wide, dtype=jnp.int32)
    to = (lane % CELLS // TS) * BOXN + (lane // CELLS) * TS + lane % TS
    perm = (to[:, None] == lane[None, :]).astype(BF)

    arrived = []
    for c in range(comps):
        outgoing = pl.pallas_call(
            lambda *refs: pick_kernel(slots, *refs),
            grid=(owners,),
            in_specs=[smem, pl.BlockSpec((tile_count, 1, slab_levels, CELLS), lambda o, c=c: (0, c, 0, 0))],
            out_specs=pl.BlockSpec((slots, slab_levels, CELLS), lambda o: (o, 0, 0)),
            out_shape=jax.ShapeDtypeStruct((total_slots, slab_levels, CELLS), BF),
            compiler_params=pltpu.CompilerParams(vmem_limit_bytes=32 << 20),
            name="pick_tiles",
        )(picked, les)
        arrived.append(lax.all_to_all(outgoing, group, split_axis=0, concat_axis=0, tiled=True))

    out = None
    for c in (1, 0, 2):
        got = arrived[c]
        edge = jnp.where(slab == 0, got[:, slab_levels - 8 :], got[:, :8])
        edge = lax.ppermute(edge, "slab", swap)
        specs = [
            smem,
            smem,
            pl.BlockSpec((total_slots, slab_levels, CELLS), lambda b: (0, 0, 0)),
            pl.BlockSpec((total_slots, 8, CELLS), lambda b: (0, 0, 0)),
            pl.BlockSpec((owners, 16, CELLS), lambda b: (0, 0, 0)),
            pl.BlockSpec((rows, 3 * count), lambda b: (0, 0)),
            pl.BlockSpec((wide, wide), lambda b: (0, 0)),
        ]
        values = [need, box_offset.reshape(-1), got, edge, wake if c == 0 else jnp.zeros_like(wake), heights, perm]
        if out is not None:
            specs.append(pl.BlockSpec(memory_space=pl.ANY))
            values.append(out)
        out = pl.pallas_call(
            lambda *refs, c=c: box_kernel(c, *refs),
            grid=(box_count,),
            in_specs=specs,
            out_specs=pl.BlockSpec((1, 1, points, BOXN * BOXN), lambda b, c=c: (b, c, 0, 0)),
            out_shape=jax.ShapeDtypeStruct((box_count, comps, points, BOXN * BOXN), BF),
            scratch_shapes=[
                pltpu.VMEM((SIDE * SIDE, count, CELLS), BF),
                pltpu.VMEM(((SIDE - 1) * rows, wide), F32),
            ],
            input_output_aliases={} if len(values) == 7 else {7: 0},
            cost_estimate=pl.CostEstimate(flops=8_000_000_000, bytes_accessed=30_000_000, transcendentals=0),
            compiler_params=pltpu.CompilerParams(vmem_limit_bytes=48 << 20),
            name="interpolate_smooth",
        )(*values)
    return out


def solution(mesh):
    placed = (
        P(("tile", "box"), None, "slab", None),
        P(),
        P(),
        P(("tile", "box"), None),
        P(("tile", "box"), "slab", None),
        P(("tile", "box"), None),
        P(("tile", "box"), None),
    )
    return jax.shard_map(
        body,
        mesh=mesh,
        in_specs=placed,
        out_specs=P(("tile", "box"), None, "slab", None),
        check_vma=False,
    )
```

```python
import jax
import jax.numpy as jnp
from jax import lax
from jax.experimental import pallas as pl
from jax.experimental.pallas import tpu as pltpu
from jax.sharding import PartitionSpec as P

BOXN = 64
TS = 16
LZ = 48
SIDE = BOXN // TS + 1
CELLS = TS * TS
FILTER_NU = 0.125
BF = jnp.bfloat16
F32 = jnp.float32


def iota(shape, dim):
    return lax.broadcasted_iota(jnp.int32, shape, dim)


def pick_kernel(slots, picked, les, out):
    owner = pl.program_id(0)
    for q in range(slots):
        out[q] = les[picked[owner * slots + q], 0]


def box_kernel(comp, need, offset, got, edge, wake, heights, perm, *rest):
    out, region, flow = rest[-3:]
    b = pl.program_id(0)
    slab = lax.axis_index("slab")
    rows = heights.shape[0]
    levels = out.shape[2]
    blocks = SIDE - 1
    shape = (CELLS, CELLS)
    src, dst = iota(shape, 0), iota(shape, 1)
    if comp == 0:
        total = jnp.zeros(wake.shape[1:], F32)
        for o in range(wake.shape[0]):
            one = wake[o]
            total = total + jnp.where(one[8:9, 128:129] == b.astype(F32), one, 0.0)
        k, r = iota((rows, total.shape[0]), 0), iota((rows, total.shape[0]), 1)
        source = jnp.where(k < levels, k // 4, jnp.where(k == levels, 9, -1))
        spread = jnp.dot(
            (source == r).astype(F32), total, precision=lax.Precision.HIGHEST, preferred_element_type=F32
        )
        k, lane = iota((rows, CELLS), 0), iota((rows, CELLS), 1)
        spread = jnp.where(lane // BOXN == jnp.where(k < levels, k % 4, 0), spread, 0.0)
        spread_hi = spread.astype(BF)
        spread_lo = (spread - spread_hi.astype(F32)).astype(BF)
    off_x, off_y = offset[2 * b], offset[2 * b + 1]

    def blend(delta, off):
        shift = off // 8
        share = (off % 8).astype(F32) / 8.0
        return jnp.where(delta == shift, 1.0 - share, jnp.where(delta == shift + 1, share, 0.0))

    gap_y, gap_x = src // TS - dst // TS, src % TS - dst % TS
    in_y = [blend(gap_y + d * TS, off_y) for d in (0, 1)]
    in_x = [blend(gap_x + d * TS, off_x) for d in (0, 1)]
    weights = jnp.concatenate([(in_y[i] * in_x[j]).astype(BF) for i in (0, 1) for j in (0, 1)], axis=0)
    for q in range(SIDE * SIDE):
        tile = need[b * SIDE * SIDE + q]
        both = jnp.concatenate([got[tile].astype(F32), edge[tile].astype(F32)], axis=0)
        region[q] = both.astype(BF)
    count = region.shape[1]
    left = jnp.concatenate(
        [
            jnp.concatenate([region[(J + i) * SIDE + I + j] for i in (0, 1) for j in (0, 1)], axis=1)
            for J in range(blocks)
            for I in range(blocks)
        ],
        axis=0,
    )
    plane = jnp.dot(left, weights, preferred_element_type=F32)
    levels_hl = heights[...]
    bands = []
    for J in range(blocks):
        if comp == 0:
            expand = (src % BOXN == dst // TS + J * TS).astype(F32).astype(BF)
            loss = jnp.dot(spread_hi, expand, preferred_element_type=F32) + jnp.dot(
                spread_lo, expand, preferred_element_type=F32
            )
        band = []
        for I in range(blocks):
            at = (J * blocks + I) * count
            part = plane[at : at + count]
            high = part.astype(BF)
            low = (part - high.astype(F32)).astype(BF)
            stack = jnp.concatenate([high, high, low], axis=0)
            value = jnp.dot(levels_hl, stack, preferred_element_type=F32)
            band.append((value - loss if comp == 0 else value).astype(BF))
        bands.append(jnp.concatenate(band, axis=1))
    flow[...] = jnp.dot(jnp.concatenate(bands, axis=0), perm[...], preferred_element_type=F32)
    points = BOXN * BOXN
    shape = (levels, points)
    row, lane = iota(shape, 0), iota(shape, 1)
    center = jnp.concatenate([flow[J * rows : J * rows + levels, :] for J in range(blocks)], axis=1)
    beside = jnp.concatenate(
        [flow[J * rows + levels : J * rows + levels + 1, :] for J in range(blocks)], axis=1
    )
    beside = jnp.broadcast_to(beside, shape)
    down = jnp.where(row == 0, jnp.where(slab == 0, center, beside), pltpu.roll(center, 1, 0))
    up = jnp.where(
        row == levels - 1, jnp.where(slab == 0, beside, center), pltpu.roll(center, levels - 1, 0)
    )
    total = down + up
    total = total + jnp.where(lane < BOXN, center, pltpu.roll(center, BOXN, 1))
    total = total + jnp.where(lane >= points - BOXN, center, pltpu.roll(center, points - BOXN, 1))
    total = total + jnp.where(lane % BOXN == 0, center, pltpu.roll(center, 1, 1))
    total = total + jnp.where(lane % BOXN == BOXN - 1, center, pltpu.roll(center, points - 1, 1))
    out[0, 0] = (center + FILTER_NU * (total - 6.0 * center)).astype(BF)


def body(les, tile_owner, tile_slot, box_offset, plane_deficit, plane_box, plane_weight):
    owners = lax.axis_size(("tile", "box"))
    my_index = lax.axis_index(("tile", "box"))
    slab = lax.axis_index("slab")
    tile_count, comps, slab_levels, _ = les.shape
    patch_count = tile_owner.shape[1]
    box_count = box_offset.shape[0]
    planes, points, _ = plane_deficit.shape
    need_count = box_count * patch_count
    slots = (need_count + owners - 1) // owners + 1
    total_slots = owners * slots
    sources = tile_owner[:, :, 0].reshape(owners, need_count)
    local_tiles = tile_slot.reshape(owners, need_count)
    from_here = (sources == my_index).astype(jnp.int32)
    slot_rank = jnp.cumsum(from_here, axis=1) - from_here
    slot_ids = jnp.arange(slots, dtype=jnp.int32)
    chosen = (from_here[:, None, :] == 1) & (slot_rank[:, None, :] == slot_ids[None, :, None])
    picked = jnp.sum(jnp.where(chosen, local_tiles[:, None, :], 0), axis=2).reshape(-1)
    wanted = lax.dynamic_slice_in_dim(sources, my_index, 1, 0)[0]
    need_ids = jnp.arange(need_count, dtype=jnp.int32)
    same_source = (wanted[:, None] == wanted[None, :]) & (need_ids[None, :] < need_ids[:, None])
    slot_of = jnp.sum(same_source.astype(jnp.int32), axis=1)
    need = wanted * slots + slot_of
    group = ("tile", "box")
    swap = [(0, 1), (1, 0)]
    smem = pl.BlockSpec(memory_space=pltpu.SMEM)

    theirs = plane_box[None] // box_count == jnp.arange(owners, dtype=jnp.int32)[:, None, None]
    gain = jnp.sum(jnp.where(theirs, plane_weight[None], 0.0), axis=2)
    tag = jnp.sum(jnp.where(theirs, plane_box[None] % box_count, 0), axis=(1, 2)).astype(F32)
    flat = plane_deficit.reshape(planes, points * BOXN // CELLS, CELLS)
    terms = gain[:, 0, None, None] * flat[0]
    for p in range(1, planes):
        terms = terms + gain[:, p, None, None] * flat[p]
    flat_rows = flat.shape[1]
    tags = jnp.broadcast_to(tag[:, None, None], (owners, 16 - flat_rows, CELLS))
    wake = lax.all_to_all(
        jnp.concatenate([terms, tags], axis=1).astype(BF), group, split_axis=0, concat_axis=0, tiled=True
    )
    rim = jnp.where(slab == 0, wake[:, flat_rows - 1, CELLS - BOXN :], wake[:, 0, :BOXN])
    rim = lax.ppermute(rim, "slab", swap)
    wake = wake.astype(F32).at[:, 9, :BOXN].set(rim.astype(F32))

    rows = points + 16
    count = slab_levels + 8
    row = jnp.arange(rows, dtype=jnp.int32)[:, None]
    height = jnp.where(row < points, slab * points + row, jnp.where(slab == 0, points, points - 1))
    num = height * (LZ - 1)
    low = num // (BOXN - 1)
    frac = (num % (BOXN - 1)).astype(F32) / float(BOXN - 1)
    col = jnp.arange(count, dtype=jnp.int32)[None, :]
    col_level = jnp.where(
        col < slab_levels, slab * slab_levels + col, jnp.where(slab == 0, col, col - 8)
    )
    mix = jnp.where(col_level == low, 1.0 - frac, jnp.where(col_level == low + 1, frac, 0.0))
    mix = jnp.where(row <= points, mix, 0.0)
    mix_hi = lax.reduce_precision(mix, 8, 7)
    mix_lo = mix - mix_hi
    heights = jnp.concatenate([mix_hi, mix_lo, mix_hi], axis=1).astype(BF)
    wide = TS * BOXN
    lane = jnp.arange(wide, dtype=jnp.int32)
    to = (lane % CELLS // TS) * BOXN + (lane // CELLS) * TS + lane % TS
    perm = (to[:, None] == lane[None, :]).astype(BF)

    arrived = []
    for c in range(comps):
        outgoing = pl.pallas_call(
            lambda *refs: pick_kernel(slots, *refs),
            grid=(owners,),
            in_specs=[smem, pl.BlockSpec((tile_count, 1, slab_levels, CELLS), lambda o, c=c: (0, c, 0, 0))],
            out_specs=pl.BlockSpec((slots, slab_levels, CELLS), lambda o: (o, 0, 0)),
            out_shape=jax.ShapeDtypeStruct((total_slots, slab_levels, CELLS), BF),
            compiler_params=pltpu.CompilerParams(vmem_limit_bytes=32 << 20),
            name="pick_tiles",
        )(picked, les)
        arrived.append(lax.all_to_all(outgoing, group, split_axis=0, concat_axis=0, tiled=True))

    out = None
    for c in (1, 0, 2):
        got = arrived[c]
        if out is not None:
            got, out = lax.optimization_barrier((got, out))
        edge = jnp.where(slab == 0, got[:, slab_levels - 8 :], got[:, :8])
        edge = lax.ppermute(edge, "slab", swap)
        specs = [
            smem,
            smem,
            pl.BlockSpec((total_slots, slab_levels, CELLS), lambda b: (0, 0, 0)),
            pl.BlockSpec((total_slots, 8, CELLS), lambda b: (0, 0, 0)),
            pl.BlockSpec((owners, 16, CELLS), lambda b: (0, 0, 0)),
            pl.BlockSpec((rows, 3 * count), lambda b: (0, 0)),
            pl.BlockSpec((wide, wide), lambda b: (0, 0)),
        ]
        values = [need, box_offset.reshape(-1), got, edge, wake if c == 0 else jnp.zeros_like(wake), heights, perm]
        if out is not None:
            specs.append(pl.BlockSpec(memory_space=pl.ANY))
            values.append(out)
        out = pl.pallas_call(
            lambda *refs, c=c: box_kernel(c, *refs),
            grid=(box_count,),
            in_specs=specs,
            out_specs=pl.BlockSpec((1, 1, points, BOXN * BOXN), lambda b, c=c: (b, c, 0, 0)),
            out_shape=jax.ShapeDtypeStruct((box_count, comps, points, BOXN * BOXN), BF),
            scratch_shapes=[
                pltpu.VMEM((SIDE * SIDE, count, CELLS), BF),
                pltpu.VMEM(((SIDE - 1) * rows, wide), F32),
            ],
            input_output_aliases={} if len(values) == 7 else {7: 0},
            cost_estimate=pl.CostEstimate(flops=8_000_000_000, bytes_accessed=30_000_000, transcendentals=0),
            compiler_params=pltpu.CompilerParams(vmem_limit_bytes=48 << 20),
            name="interpolate_smooth",
        )(*values)
    return out


def solution(mesh):
    placed = (
        P(("tile", "box"), None, "slab", None),
        P(),
        P(),
        P(("tile", "box"), None),
        P(("tile", "box"), "slab", None),
        P(("tile", "box"), None),
        P(("tile", "box"), None),
    )
    return jax.shard_map(
        body,
        mesh=mesh,
        in_specs=placed,
        out_specs=P(("tile", "box"), None, "slab", None),
        check_vma=False,
    )
```

```python
import jax
import jax.numpy as jnp
from jax import lax
from jax.experimental import pallas as pl
from jax.experimental.pallas import tpu as pltpu
from jax.sharding import PartitionSpec as P

BOXN = 64
TS = 16
LZ = 48
SIDE = BOXN // TS + 1
CELLS = TS * TS
FILTER_NU = 0.125
BF = jnp.bfloat16
F32 = jnp.float32


def iota(shape, dim):
    return lax.broadcasted_iota(jnp.int32, shape, dim)


def pick_kernel(slots, picked, les, out):
    owner = pl.program_id(0)
    for q in range(slots):
        out[q] = les[picked[owner * slots + q]]


def box_kernel(comp, need, offset, got, edge, wake, heights, perm, *rest):
    out, region, flow = rest[-3:]
    b = pl.program_id(0)
    slab = lax.axis_index("slab")
    rows = heights.shape[0]
    levels = out.shape[2]
    blocks = SIDE - 1
    shape = (CELLS, CELLS)
    src, dst = iota(shape, 0), iota(shape, 1)
    if comp == 0:
        total = jnp.zeros(wake.shape[1:], F32)
        for o in range(wake.shape[0]):
            one = wake[o]
            total = total + jnp.where(one[8:9, 128:129] == b.astype(F32), one, 0.0)
        k, r = iota((rows, total.shape[0]), 0), iota((rows, total.shape[0]), 1)
        source = jnp.where(k < levels, k // 4, jnp.where(k == levels, 9, -1))
        spread = jnp.dot(
            (source == r).astype(F32), total, precision=lax.Precision.HIGHEST, preferred_element_type=F32
        )
        k, lane = iota((rows, CELLS), 0), iota((rows, CELLS), 1)
        spread = jnp.where(lane // BOXN == jnp.where(k < levels, k % 4, 0), spread, 0.0)
        spread_hi = spread.astype(BF)
        spread_lo = (spread - spread_hi.astype(F32)).astype(BF)
    off_x, off_y = offset[2 * b], offset[2 * b + 1]

    def blend(delta, off):
        shift = off // 8
        share = (off % 8).astype(F32) / 8.0
        return jnp.where(delta == shift, 1.0 - share, jnp.where(delta == shift + 1, share, 0.0))

    gap_y, gap_x = src // TS - dst // TS, src % TS - dst % TS
    in_y = [blend(gap_y + d * TS, off_y) for d in (0, 1)]
    in_x = [blend(gap_x + d * TS, off_x) for d in (0, 1)]
    weights = jnp.concatenate([(in_y[i] * in_x[j]).astype(BF) for i in (0, 1) for j in (0, 1)], axis=0)
    for q in range(SIDE * SIDE):
        tile = need[b * SIDE * SIDE + q]
        both = jnp.concatenate([got[tile, 0].astype(F32), edge[tile].astype(F32)], axis=0)
        region[q] = both.astype(BF)
    count = region.shape[1]
    left = jnp.concatenate(
        [
            jnp.concatenate([region[(J + i) * SIDE + I + j] for i in (0, 1) for j in (0, 1)], axis=1)
            for J in range(blocks)
            for I in range(blocks)
        ],
        axis=0,
    )
    plane = jnp.dot(left, weights, preferred_element_type=F32)
    levels_hl = heights[...]
    bands = []
    for J in range(blocks):
        if comp == 0:
            expand = (src % BOXN == dst // TS + J * TS).astype(F32).astype(BF)
            loss = jnp.dot(spread_hi, expand, preferred_element_type=F32) + jnp.dot(
                spread_lo, expand, preferred_element_type=F32
            )
        band = []
        for I in range(blocks):
            at = (J * blocks + I) * count
            part = plane[at : at + count]
            high = part.astype(BF)
            low = (part - high.astype(F32)).astype(BF)
            stack = jnp.concatenate([high, high, low], axis=0)
            value = jnp.dot(levels_hl, stack, preferred_element_type=F32)
            band.append((value - loss if comp == 0 else value).astype(BF))
        bands.append(jnp.concatenate(band, axis=1))
    flow[...] = jnp.dot(jnp.concatenate(bands, axis=0), perm[...], preferred_element_type=F32)
    points = BOXN * BOXN
    shape = (levels, points)
    row, lane = iota(shape, 0), iota(shape, 1)
    center = jnp.concatenate([flow[J * rows : J * rows + levels, :] for J in range(blocks)], axis=1)
    beside = jnp.concatenate(
        [flow[J * rows + levels : J * rows + levels + 1, :] for J in range(blocks)], axis=1
    )
    beside = jnp.broadcast_to(beside, shape)
    down = jnp.where(row == 0, jnp.where(slab == 0, center, beside), pltpu.roll(center, 1, 0))
    up = jnp.where(
        row == levels - 1, jnp.where(slab == 0, beside, center), pltpu.roll(center, levels - 1, 0)
    )
    total = down + up
    total = total + jnp.where(lane < BOXN, center, pltpu.roll(center, BOXN, 1))
    total = total + jnp.where(lane >= points - BOXN, center, pltpu.roll(center, points - BOXN, 1))
    total = total + jnp.where(lane % BOXN == 0, center, pltpu.roll(center, 1, 1))
    total = total + jnp.where(lane % BOXN == BOXN - 1, center, pltpu.roll(center, points - 1, 1))
    out[0, 0] = (center + FILTER_NU * (total - 6.0 * center)).astype(BF)


def body(les, tile_owner, tile_slot, box_offset, plane_deficit, plane_box, plane_weight):
    owners = lax.axis_size(("tile", "box"))
    my_index = lax.axis_index(("tile", "box"))
    slab = lax.axis_index("slab")
    tile_count, comps, slab_levels, _ = les.shape
    patch_count = tile_owner.shape[1]
    box_count = box_offset.shape[0]
    planes, points, _ = plane_deficit.shape
    need_count = box_count * patch_count
    slots = (need_count + owners - 1) // owners + 1
    total_slots = owners * slots
    sources = tile_owner[:, :, 0].reshape(owners, need_count)
    local_tiles = tile_slot.reshape(owners, need_count)
    from_here = (sources == my_index).astype(jnp.int32)
    slot_rank = jnp.cumsum(from_here, axis=1) - from_here
    slot_ids = jnp.arange(slots, dtype=jnp.int32)
    chosen = (from_here[:, None, :] == 1) & (slot_rank[:, None, :] == slot_ids[None, :, None])
    picked = jnp.sum(jnp.where(chosen, local_tiles[:, None, :], 0), axis=2).reshape(-1)
    wanted = lax.dynamic_slice_in_dim(sources, my_index, 1, 0)[0]
    need_ids = jnp.arange(need_count, dtype=jnp.int32)
    same_source = (wanted[:, None] == wanted[None, :]) & (need_ids[None, :] < need_ids[:, None])
    slot_of = jnp.sum(same_source.astype(jnp.int32), axis=1)
    need = wanted * slots + slot_of
    group = ("tile", "box")
    swap = [(0, 1), (1, 0)]
    smem = pl.BlockSpec(memory_space=pltpu.SMEM)

    theirs = plane_box[None] // box_count == jnp.arange(owners, dtype=jnp.int32)[:, None, None]
    gain = jnp.sum(jnp.where(theirs, plane_weight[None], 0.0), axis=2)
    tag = jnp.sum(jnp.where(theirs, plane_box[None] % box_count, 0), axis=(1, 2)).astype(F32)
    flat = plane_deficit.reshape(planes, points * BOXN // CELLS, CELLS)
    terms = gain[:, 0, None, None] * flat[0]
    for p in range(1, planes):
        terms = terms + gain[:, p, None, None] * flat[p]
    flat_rows = flat.shape[1]
    tags = jnp.broadcast_to(tag[:, None, None], (owners, 16 - flat_rows, CELLS))
    wake = jnp.concatenate([terms, tags], axis=1).astype(BF)

    rows = points + 16
    count = slab_levels + 8
    row = jnp.arange(rows, dtype=jnp.int32)[:, None]
    height = jnp.where(row < points, slab * points + row, jnp.where(slab == 0, points, points - 1))
    num = height * (LZ - 1)
    low = num // (BOXN - 1)
    frac = (num % (BOXN - 1)).astype(F32) / float(BOXN - 1)
    col = jnp.arange(count, dtype=jnp.int32)[None, :]
    col_level = jnp.where(
        col < slab_levels, slab * slab_levels + col, jnp.where(slab == 0, col, col - 8)
    )
    mix = jnp.where(col_level == low, 1.0 - frac, jnp.where(col_level == low + 1, frac, 0.0))
    mix = jnp.where(row <= points, mix, 0.0)
    mix_hi = lax.reduce_precision(mix, 8, 7)
    mix_lo = mix - mix_hi
    heights = jnp.concatenate([mix_hi, mix_lo, mix_hi], axis=1).astype(BF)
    wide = TS * BOXN
    lane = jnp.arange(wide, dtype=jnp.int32)
    to = (lane % CELLS // TS) * BOXN + (lane // CELLS) * TS + lane % TS
    perm = (to[:, None] == lane[None, :]).astype(BF)

    def picks(start, width):
        return pl.pallas_call(
            lambda *refs: pick_kernel(slots, *refs),
            grid=(owners,),
            in_specs=[
                smem,
                pl.BlockSpec((tile_count, width, slab_levels, CELLS), lambda o: (0, start // width, 0, 0)),
            ],
            out_specs=pl.BlockSpec((slots, width, slab_levels, CELLS), lambda o: (o, 0, 0, 0)),
            out_shape=jax.ShapeDtypeStruct((total_slots, width, slab_levels, CELLS), BF),
            compiler_params=pltpu.CompilerParams(vmem_limit_bytes=32 << 20),
            name="pick_tiles",
        )(picked, les)

    def exchange(x):
        return lax.all_to_all(x, group, split_axis=0, concat_axis=0, tiled=True)

    pair = exchange(picks(0, 2))
    pair, wake = lax.optimization_barrier((pair, wake))
    wake = exchange(wake)
    single, wake = lax.optimization_barrier((picks(2, 1), wake))
    single = exchange(single)
    rim = jnp.where(slab == 0, wake[:, flat_rows - 1, CELLS - BOXN :], wake[:, 0, :BOXN])
    rim = lax.ppermute(rim, "slab", swap)
    wake = wake.astype(F32).at[:, 9, :BOXN].set(rim.astype(F32))

    out = None
    for c in (1, 0, 2):
        got, at = (single, 0) if c == 2 else (pair, c)
        if out is not None:
            got, out = lax.optimization_barrier((got, out))
            pair = got if c == 0 else pair
        edge = jnp.where(slab == 0, got[:, at, slab_levels - 8 :], got[:, at, :8])
        edge = lax.ppermute(edge, "slab", swap)
        specs = [
            smem,
            smem,
            pl.BlockSpec((total_slots, 1, slab_levels, CELLS), lambda b, at=at: (0, at, 0, 0)),
            pl.BlockSpec((total_slots, 8, CELLS), lambda b: (0, 0, 0)),
            pl.BlockSpec((owners, 16, CELLS), lambda b: (0, 0, 0)),
            pl.BlockSpec((rows, 3 * count), lambda b: (0, 0)),
            pl.BlockSpec((wide, wide), lambda b: (0, 0)),
        ]
        values = [need, box_offset.reshape(-1), got, edge, wake if c == 0 else jnp.zeros_like(wake), heights, perm]
        if out is not None:
            specs.append(pl.BlockSpec(memory_space=pl.ANY))
            values.append(out)
        out = pl.pallas_call(
            lambda *refs, c=c: box_kernel(c, *refs),
            grid=(box_count,),
            in_specs=specs,
            out_specs=pl.BlockSpec((1, 1, points, BOXN * BOXN), lambda b, c=c: (b, c, 0, 0)),
            out_shape=jax.ShapeDtypeStruct((box_count, comps, points, BOXN * BOXN), BF),
            scratch_shapes=[
                pltpu.VMEM((SIDE * SIDE, count, CELLS), BF),
                pltpu.VMEM(((SIDE - 1) * rows, wide), F32),
            ],
            input_output_aliases={} if len(values) == 7 else {7: 0},
            cost_estimate=pl.CostEstimate(flops=8_000_000_000, bytes_accessed=30_000_000, transcendentals=0),
            compiler_params=pltpu.CompilerParams(vmem_limit_bytes=48 << 20),
            name="interpolate_smooth",
        )(*values)
    return out


def solution(mesh):
    placed = (
        P(("tile", "box"), None, "slab", None),
        P(),
        P(),
        P(("tile", "box"), None),
        P(("tile", "box"), "slab", None),
        P(("tile", "box"), None),
        P(("tile", "box"), None),
    )
    return jax.shard_map(
        body,
        mesh=mesh,
        in_specs=placed,
        out_specs=P(("tile", "box"), None, "slab", None),
        check_vma=False,
    )
```
